512 devices in a mesh: row: 32 (over x, y, core), col: 16 (over z).
Axes of the slice: x: 4, y: 4, z: 16, core: 2. Of those that a mesh axis runs over, the one named last changes fastest.
Arguments:
- rhs_head: float32 [2, 2048, 4096], P(None, 'row', 'col'), may hold values from -6 to 6
- rhs_tail: float32 [14336, 4096], P('row', 'col'), may hold values from -6 to 6
- diag_inv: float32 [2, 2048, 2048], P(None, 'row'), as said below
- factor_cross: float32 [2048, 2048], P('row', 'col'), may hold values from -0.125 to 0.125
- factor_tail: float32 [14336, 2, 2048], P('row', None, 'col'), may hold values from -0.09375 to 0.09375
Outputs:
- solved: float32 [2, 2048, 4096], P(None, 'row', 'col')
- updated_tail: float32 [14336, 4096], P('row', 'col')
The draws below stay inside these ranges and needn't reach their ends.
Inputs may be any that keep to these rules, and one draw needn't show every extreme that they name: diag_inv[k] is lower triangular with diagonal entries from 0.5 to 1.5.
All inputs are finite; a program needn't handle non-finite values.
Results may differ from the reference program's by a relative error of at most 0.000092.
Values sent between devices are 32-bit elements; how exact they have to be, the bound alone decides.
No kernel may reach another device: no remote copies, remote signals or barrier semaphores. Data moves between devices by JAX's collectives and lax.ppermute only.
A program may use at most 64 MiB of HBM per device.

```python
import math
import jax
import jax.numpy as jnp
from jax import lax

PB = 2048
TROWS = 14336
NRHS = 4096


def draw_diag_inv(key, part):
    key = jax.random.fold_in(key, 7)
    below_key, diag_key = jax.random.split(key)
    below = jnp.clip(jax.random.normal(below_key, (2, PB, PB), jnp.float32), -4.0, 4.0) / math.sqrt(PB)
    below = jnp.tril(below, -1)
    diagonal = jax.random.uniform(diag_key, (2, PB), jnp.float32, 0.5, 1.5)
    return below + diagonal[:, :, None] * jnp.eye(PB, dtype=jnp.float32)


def shard_levels(own_key, shape, cuts, least, largest):
    factor_of, own = 1.0, jax.random.fold_in(own_key, 6)
    for position, blocks in cuts:
        heights = jnp.exp(jax.random.uniform(jax.random.fold_in(own, position), (blocks,), jnp.float32, least / len(cuts), largest / len(cuts)))
        factor_of = factor_of * jnp.repeat(heights, shape[position] // blocks).reshape([-1 if axis == position else 1 for axis in range(len(shape))])
    return factor_of


def noise(key, shape, scale, most, cuts=(), kind=jnp.bfloat16):
    entries = scale * jax.random.normal(key, shape, jnp.float32)
    if cuts:
        entries = entries * shard_levels(key, shape, cuts, -0.22, 0.18)
    return jnp.clip(entries, -most, most).astype(kind)


def setup_inputs(seed: int = 0) -> dict:
    seeds = jax.random.split(jax.random.key(seed), 6)
    rhs_head = noise(seeds[0], (2, PB, NRHS), 1.0, 6.0, ((1, 32), (2, 16)), jnp.float32)
    rhs_tail = noise(seeds[1], (TROWS, NRHS), 1.0, 6.0, ((0, 32), (1, 16)), jnp.float32)
    diag_inv = draw_diag_inv(jax.random.fold_in(seeds[5], 71), 0)
    factor_cross = noise(seeds[3], (PB, PB), PB ** -0.5, 0.125, ((0, 32), (1, 16)), jnp.float32)
    factor_tail = noise(seeds[4], (TROWS, 2, PB), (2 * PB) ** -0.5, 0.09375, ((0, 32), (2, 16)), jnp.float32)
    return dict(rhs_head=rhs_head, rhs_tail=rhs_tail, diag_inv=diag_inv, factor_cross=factor_cross, factor_tail=factor_tail)


def product(matrix, operand):
    return jnp.dot(matrix, operand, precision=lax.Precision.HIGHEST, preferred_element_type=jnp.float32)


def reference(rhs_head, rhs_tail, diag_inv, factor_cross, factor_tail):
    first_solved = product(diag_inv[0], rhs_head[0])
    second_head = rhs_head[1] - product(factor_cross, first_solved)
    second_solved = product(diag_inv[1], second_head)
    solved = jnp.stack([first_solved, second_solved])
    updated_tail = rhs_tail - product(factor_tail[:, 0, :], first_solved) - product(factor_tail[:, 1, :], second_solved)
    return solved, updated_tail
```

```python
import functools

import jax
import jax.numpy as jnp
from jax import lax
from jax.experimental import pallas as pl
from jax.experimental.pallas import tpu as pltpu
from jax.sharding import PartitionSpec as P

CORES = 2
TAIL_STEPS = 4


def swap(value):
    rows = lax.axis_size("row")
    return lax.ppermute(value, "row", [(i, i ^ 1) for i in range(rows)])


def gather_chips(copies):
    rows = lax.axis_size("row")
    groups = [list(range(core, rows, CORES)) for core in range(CORES)]
    blocks = lax.all_to_all(copies, "row", 0, 0, axis_index_groups=groups, tiled=True)
    return blocks.reshape(-1, blocks.shape[-1])


def gather_half(copies):
    chips, cores, rows, half = copies.shape
    return lax.all_to_all(copies.reshape(chips * cores, rows, half), "row", 0, 0, tiled=True).reshape(-1, half)


def gather_panels(block):
    planes = lax.axis_size("col")
    return lax.all_to_all(jnp.broadcast_to(block[None], (planes,) + block.shape), "col", 0, 0, tiled=True)


def split(value):
    high = value.astype(jnp.bfloat16)
    low = (value - high.astype(jnp.float32)).astype(jnp.bfloat16)
    return high, low


def product(left, right):
    left_high, left_low = split(left)
    right_high, right_low = split(right)
    dot = functools.partial(jnp.dot, preferred_element_type=jnp.float32)
    return dot(left_high, right_high) + (dot(left_high, right_low) + dot(left_low, right_high))


def in_order(own, other, axis):
    first = lax.axis_index("row") % CORES == 0
    return jnp.concatenate([jnp.where(first, own, other), jnp.where(first, other, own)], axis=axis)


def spread(value, out):
    for chip in range(out.shape[0]):
        out[chip] = value


def prepare_kernel(heads, copies, keep, send):
    half = keep.shape[1]
    halves = [heads[0][:, core * half : (core + 1) * half] for core in range(CORES)]
    for chip in range(copies.shape[0]):
        for core in range(CORES):
            copies[chip, core] = halves[core]
    first = lax.axis_index("row") % CORES == 0
    left, right = heads[1][:, :half], heads[1][:, half:]
    keep[...] = jnp.where(first, left, right)
    send[...] = jnp.where(first, right, left)


def solve_kernel(own, other, operand, out):
    spread(product(in_order(own[0], other[0], 0), operand[...]), out)


def cross_kernel(own, other, head, head_other, operand, out):
    row_of = lambda blocks: jnp.concatenate([blocks[i] for i in range(blocks.shape[0])], axis=1)
    left = in_order(row_of(own), row_of(other), 0)
    spread(in_order(head[...], head_other[...], 0) - product(left, operand[...]), out)


def tail_kernel(tail, factor, first, first_other, second, second_other, out, solved, total):
    step = pl.program_id(0)
    row = lax.axis_index("row")
    own_rows, depth, rows = solved.shape[1], factor.shape[2], out.shape[0]
    per_step = first.shape[0] // own_rows

    @pl.when(step == row // per_step)
    def _():
        at = pl.ds(pl.multiple_of((row % per_step) * own_rows, own_rows), own_rows)
        solved[0] = in_order(first[at, :], first_other[at, :], 1)
        solved[1] = in_order(second[at, :], second_other[at, :], 1)

    left, right = [], []
    for block in range(factor.shape[0]):
        at = pl.ds(block * depth, depth)
        for panel, (own, other) in enumerate(((first, first_other), (second, second_other))):
            left.append(factor[block, pl.ds(panel, rows, stride=2), :])
            right.append(jnp.concatenate([own[at, :], other[at, :]], axis=1))
    part = product(jnp.concatenate(left, axis=1), jnp.concatenate(right, axis=0))

    @pl.when(step == 0)
    def _():
        total[...] = part

    @pl.when(step > 0)
    def _():
        total[...] += part

    @pl.when(step == pl.num_programs(0) - 1)
    def _():
        half = out.shape[1] // 2
        out[...] = tail[...] - in_order(total[:, :half], total[:, half:], 1)


def params(mib):
    return pltpu.CompilerParams(vmem_limit_bytes=mib * 1024 * 1024)


def estimate(flops, size):
    return pl.CostEstimate(flops=flops, bytes_accessed=size, transcendentals=0)


def prepare(heads):
    _, rows, columns = heads.shape
    half = columns // CORES
    chips = lax.axis_size("row") // CORES
    part = jax.ShapeDtypeStruct((rows, half), jnp.float32)
    return pl.pallas_call(
        prepare_kernel,
        out_shape=(jax.ShapeDtypeStruct((chips, CORES, rows, half), jnp.float32), part, part),
        compiler_params=params(8),
        cost_estimate=estimate(0, 4 * (chips + 3) * rows * columns),
    )(heads)


def solve_chip(panel, own, other, operand):
    _, rows, depth = own.shape
    columns = operand.shape[1]
    chips = lax.axis_size("row") // CORES
    inverse = pl.BlockSpec((1, rows, depth), lambda step: (panel, 0, 0))
    shape = (chips, CORES * rows, columns)
    return pl.pallas_call(
        solve_kernel,
        grid=(1,),
        in_specs=[inverse, inverse, pl.BlockSpec(operand.shape, lambda step: (0, 0))],
        out_specs=pl.BlockSpec(shape, lambda step: (0, 0, 0)),
        out_shape=jax.ShapeDtypeStruct(shape, jnp.float32),
        compiler_params=params(16),
        cost_estimate=estimate(12 * rows * depth * columns, 4 * depth * (2 * rows + 2 * columns)),
    )(own, other, operand)


def cross_chip(own, other, head, head_other, operand):
    _, rows, _ = own.shape
    depth, columns = operand.shape
    chips = lax.axis_size("row") // CORES
    return pl.pallas_call(
        cross_kernel,
        out_shape=jax.ShapeDtypeStruct((chips, CORES * rows, columns), jnp.float32),
        compiler_params=params(16),
        cost_estimate=estimate(12 * rows * depth * columns, 4 * depth * (2 * rows + 2 * columns)),
    )(own, other, head, head_other, operand)


def tail_rows(tail, factor, halves):
    rows, columns = tail.shape
    blocks, double, width = factor.shape
    depth, half = halves[0].shape
    own_rows = depth // lax.axis_size("row")
    whole = lambda shape: pl.BlockSpec(shape, lambda step: (0,) * len(shape))
    shapes = [
        jax.ShapeDtypeStruct((rows, columns), jnp.float32),
        jax.ShapeDtypeStruct((2, own_rows, columns), jnp.float32),
    ]
    return pl.pallas_call(
        tail_kernel,
        grid=(TAIL_STEPS,),
        in_specs=[
            whole(tail.shape),
            pl.BlockSpec((blocks // TAIL_STEPS, double, width), lambda step: (step, 0, 0)),
        ]
        + [pl.BlockSpec((depth // TAIL_STEPS, half), lambda step: (step, 0)) for _ in halves],
        out_specs=[whole(shape.shape) for shape in shapes],
        out_shape=shapes,
        scratch_shapes=[pltpu.VMEM((rows, columns), jnp.float32)],
        compiler_params=params(55),
        cost_estimate=estimate(12 * rows * depth * columns, 4 * blocks * double * width),
    )(tail, factor, *halves)


def local(rhs_head, rhs_tail, diag_inv, factor_cross, factor_tail):
    rows, _, width = factor_tail.shape
    factor = lax.all_gather(factor_tail.reshape(2 * rows, width), "col", axis=0)
    copies, head, head_other = prepare(rhs_head)
    copies, diag_inv, factor_cross, head_other = lax.optimization_barrier(
        (copies, diag_inv, factor_cross, head_other)
    )
    first_head = gather_half(copies)
    inverse_other = swap(diag_inv)
    head_other = swap(head_other)
    cross = gather_panels(factor_cross)
    cross_other = swap(cross)

    first = gather_chips(solve_chip(0, diag_inv, inverse_other, first_head))
    second_head = gather_chips(cross_chip(cross, cross_other, head, head_other, first))
    second = gather_chips(solve_chip(1, diag_inv, inverse_other, second_head))
    tail, solved = tail_rows(rhs_tail, factor, (first, swap(first), second, swap(second)))
    return solved, tail


def solution(mesh):
    return jax.shard_map(
        local,
        mesh=mesh,
        in_specs=(
            P(None, "row", "col"),
            P("row", "col"),
            P(None, "row", None),
            P("row", "col"),
            P("row", None, "col"),
        ),
        out_specs=(P(None, "row", "col"), P("row", "col")),
        check_vma=False,
    )
```

```python
import functools

import jax
import jax.numpy as jnp
from jax import lax
from jax.experimental import pallas as pl
from jax.experimental.pallas import tpu as pltpu
from jax.sharding import PartitionSpec as P

CORES = 2
TAIL_STEPS = 4


def swap(value):
    rows = lax.axis_size("row")
    return lax.ppermute(value, "row", [(i, i ^ 1) for i in range(rows)])


def gather_chips(copies):
    rows = lax.axis_size("row")
    groups = [list(range(core, rows, CORES)) for core in range(CORES)]
    blocks = lax.all_to_all(copies, "row", 0, 0, axis_index_groups=groups, tiled=True)
    return blocks.reshape(-1, blocks.shape[-1])


def gather_half(copies):
    chips, cores, rows, half = copies.shape
    return lax.all_to_all(copies.reshape(chips * cores, rows, half), "row", 0, 0, tiled=True).reshape(-1, half)


def split(value):
    high = value.astype(jnp.bfloat16)
    low = (value - high.astype(jnp.float32)).astype(jnp.bfloat16)
    return high, low


def product(left, right):
    left_high, left_low = split(left)
    right_high, right_low = split(right)
    dot = functools.partial(jnp.dot, preferred_element_type=jnp.float32)
    return dot(left_high, right_high) + (dot(left_high, right_low) + dot(left_low, right_high))


def in_order(own, other, axis):
    first = lax.axis_index("row") % CORES == 0
    return jnp.concatenate([jnp.where(first, own, other), jnp.where(first, other, own)], axis=axis)


def spread(value, out):
    for chip in range(out.shape[0]):
        out[chip] = value


def prepare_kernel(heads, copies, keep, send):
    half = keep.shape[1]
    halves = [heads[0][:, core * half : (core + 1) * half] for core in range(CORES)]
    for chip in range(copies.shape[0]):
        for core in range(CORES):
            copies[chip, core] = halves[core]
    first = lax.axis_index("row") % CORES == 0
    left, right = heads[1][:, :half], heads[1][:, half:]
    keep[...] = jnp.where(first, left, right)
    send[...] = jnp.where(first, right, left)


def solve_kernel(own, other, operand, out):
    spread(product(in_order(own[0], other[0], 0), operand[...]), out)


def cross_kernel(own, other, head, head_other, operand, out):
    row_of = lambda blocks: jnp.concatenate([blocks[i] for i in range(blocks.shape[0])], axis=1)
    left = in_order(row_of(own), row_of(other), 0)
    spread(in_order(head[...], head_other[...], 0) - product(left, operand[...]), out)


def tail_kernel(tail, factor, first, first_other, second, second_other, out, solved, total):
    step = pl.program_id(0)
    row = lax.axis_index("row")
    own_rows, depth, rows = solved.shape[1], factor.shape[2], out.shape[0]
    per_step = first.shape[0] // own_rows

    @pl.when(step == row // per_step)
    def _():
        at = pl.ds(pl.multiple_of((row % per_step) * own_rows, own_rows), own_rows)
        solved[0] = in_order(first[at, :], first_other[at, :], 1)
        solved[1] = in_order(second[at, :], second_other[at, :], 1)

    left, right = [], []
    for block in range(factor.shape[0]):
        at = pl.ds(block * depth, depth)
        for panel, (own, other) in enumerate(((first, first_other), (second, second_other))):
            left.append(factor[block, pl.ds(panel, rows, stride=2), :])
            right.append(jnp.concatenate([own[at, :], other[at, :]], axis=1))
    part = product(jnp.concatenate(left, axis=1), jnp.concatenate(right, axis=0))

    @pl.when(step == 0)
    def _():
        total[...] = part

    @pl.when(step > 0)
    def _():
        total[...] += part

    @pl.when(step == pl.num_programs(0) - 1)
    def _():
        half = out.shape[1] // 2
        out[...] = tail[...] - in_order(total[:, :half], total[:, half:], 1)


def params(mib):
    return pltpu.CompilerParams(vmem_limit_bytes=mib * 1024 * 1024)


def estimate(flops, size):
    return pl.CostEstimate(flops=flops, bytes_accessed=size, transcendentals=0)


def prepare(heads):
    _, rows, columns = heads.shape
    half = columns // CORES
    chips = lax.axis_size("row") // CORES
    part = jax.ShapeDtypeStruct((rows, half), jnp.float32)
    return pl.pallas_call(
        prepare_kernel,
        out_shape=(jax.ShapeDtypeStruct((chips, CORES, rows, half), jnp.float32), part, part),
        compiler_params=params(8),
        cost_estimate=estimate(0, 4 * (chips + 3) * rows * columns),
    )(heads)


def solve_chip(panel, own, other, operand):
    _, rows, depth = own.shape
    columns = operand.shape[1]
    chips = lax.axis_size("row") // CORES
    inverse = pl.BlockSpec((1, rows, depth), lambda step: (panel, 0, 0))
    shape = (chips, CORES * rows, columns)
    return pl.pallas_call(
        solve_kernel,
        grid=(1,),
        in_specs=[inverse, inverse, pl.BlockSpec(operand.shape, lambda step: (0, 0))],
        out_specs=pl.BlockSpec(shape, lambda step: (0, 0, 0)),
        out_shape=jax.ShapeDtypeStruct(shape, jnp.float32),
        compiler_params=params(16),
        cost_estimate=estimate(12 * rows * depth * columns, 4 * depth * (2 * rows + 2 * columns)),
    )(own, other, operand)


def cross_chip(own, other, head, head_other, operand):
    _, rows, _ = own.shape
    depth, columns = operand.shape
    chips = lax.axis_size("row") // CORES
    return pl.pallas_call(
        cross_kernel,
        out_shape=jax.ShapeDtypeStruct((chips, CORES * rows, columns), jnp.float32),
        compiler_params=params(16),
        cost_estimate=estimate(12 * rows * depth * columns, 4 * depth * (2 * rows + 2 * columns)),
    )(own, other, head, head_other, operand)


def tail_rows(tail, factor, halves):
    rows, columns = tail.shape
    blocks, double, width = factor.shape
    depth, half = halves[0].shape
    own_rows = depth // lax.axis_size("row")
    whole = lambda shape: pl.BlockSpec(shape, lambda step: (0,) * len(shape))
    shapes = [
        jax.ShapeDtypeStruct((rows, columns), jnp.float32),
        jax.ShapeDtypeStruct((2, own_rows, columns), jnp.float32),
    ]
    return pl.pallas_call(
        tail_kernel,
        grid=(TAIL_STEPS,),
        in_specs=[
            whole(tail.shape),
            pl.BlockSpec((blocks // TAIL_STEPS, double, width), lambda step: (step, 0, 0)),
        ]
        + [pl.BlockSpec((depth // TAIL_STEPS, half), lambda step: (step, 0)) for _ in halves],
        out_specs=[whole(shape.shape) for shape in shapes],
        out_shape=shapes,
        scratch_shapes=[pltpu.VMEM((rows, columns), jnp.float32)],
        compiler_params=params(55),
        cost_estimate=estimate(12 * rows * depth * columns, 4 * blocks * double * width),
    )(tail, factor, *halves)


def local(rhs_head, rhs_tail, diag_inv, factor_cross, factor_tail):
    rows, _, width = factor_tail.shape
    factor = lax.all_gather(factor_tail.reshape(2 * rows, width), "col", axis=0)
    copies, head, head_other = prepare(rhs_head)
    copies, diag_inv, factor_cross, head_other = lax.optimization_barrier(
        (copies, diag_inv, factor_cross, head_other)
    )
    first_head = gather_half(copies)
    inverse_other = swap(diag_inv)
    head_other = swap(head_other)
    cross = lax.all_gather(factor_cross, "col", axis=0)
    first_head, cross = lax.optimization_barrier((first_head, cross))
    cross_other = swap(cross)

    first = gather_chips(solve_chip(0, diag_inv, inverse_other, first_head))
    second_head = gather_chips(cross_chip(cross, cross_other, head, head_other, first))
    second = gather_chips(solve_chip(1, diag_inv, inverse_other, second_head))
    tail, solved = tail_rows(rhs_tail, factor, (first, swap(first), second, swap(second)))
    return solved, tail


def solution(mesh):
    return jax.shard_map(
        local,
        mesh=mesh,
        in_specs=(
            P(None, "row", "col"),
            P("row", "col"),
            P(None, "row", None),
            P("row", "col"),
            P("row", None, "col"),
        ),
        out_specs=(P(None, "row", "col"), P("row", "col")),
        check_vma=False,
    )
```

```python
import functools

import jax
import jax.numpy as jnp
from jax import lax
from jax.experimental import pallas as pl
from jax.experimental.pallas import tpu as pltpu
from jax.sharding import PartitionSpec as P

CORES = 2
TAIL_STEPS = 4


def swap(value):
    rows = lax.axis_size("row")
    return lax.ppermute(value, "row", [(i, i ^ 1) for i in range(rows)])


def gather_chips(copies):
    rows = lax.axis_size("row")
    groups = [list(range(core, rows, CORES)) for core in range(CORES)]
    blocks = lax.all_to_all(copies, "row", 0, 0, axis_index_groups=groups, tiled=True)
    return blocks.reshape(-1, blocks.shape[-1])


def gather_half(copies):
    chips, cores, rows, half = copies.shape
    return lax.all_to_all(copies.reshape(chips * cores, rows, half), "row", 0, 0, tiled=True).reshape(-1, half)


def split(value):
    high = value.astype(jnp.bfloat16)
    low = (value - high.astype(jnp.float32)).astype(jnp.bfloat16)
    return high, low


def product(left, right):
    left_high, left_low = split(left)
    right_high, right_low = split(right)
    dot = functools.partial(jnp.dot, preferred_element_type=jnp.float32)
    return dot(left_high, right_high) + (dot(left_high, right_low) + dot(left_low, right_high))


def in_order(own, other, axis):
    first = lax.axis_index("row") % CORES == 0
    return jnp.concatenate([jnp.where(first, own, other), jnp.where(first, other, own)], axis=axis)


def spread(value, out):
    for chip in range(out.shape[0]):
        out[chip] = value


def prepare_kernel(heads, cross, first_copies, second_copies, cross_copies):
    half = first_copies.shape[3]
    for chip in range(cross_copies.shape[0]):
        cross_copies[chip] = cross[...]
        for core in range(CORES):
            columns = slice(core * half, (core + 1) * half)
            first_copies[chip, core] = heads[0][:, columns]
            second_copies[chip, core] = heads[1][:, columns]


def solve_kernel(own, other, operand, out):
    spread(product(in_order(own[0], other[0], 0), operand[...]), out)


def cross_kernel(own, other, cross, keep, send):
    right = []
    for chip in range(cross.shape[0]):
        right.append(in_order(cross[chip], jnp.zeros_like(cross[chip]), 0))
    part = product(jnp.concatenate([own[0], other[0]], axis=0), jnp.concatenate(right, axis=0))
    rows = keep.shape[0]
    keep[...] = part[:rows]
    send[...] = part[rows:]


def second_kernel(own, other, cross, cross_other, operand, first, out):
    row_of = lambda blocks: jnp.concatenate([blocks[i] for i in range(blocks.shape[0])], axis=1)
    solved = product(in_order(own[0], other[0], 0), operand[...])
    spread(solved - product(in_order(row_of(cross), row_of(cross_other), 0), first[...]), out)


def tail_kernel(tail, factor, first, first_other, second, second_other, out, solved, total):
    step = pl.program_id(0)
    row = lax.axis_index("row")
    own_rows, depth, rows = solved.shape[1], factor.shape[2], out.shape[0]
    per_step = first.shape[0] // own_rows

    @pl.when(step == row // per_step)
    def _():
        at = pl.ds(pl.multiple_of((row % per_step) * own_rows, own_rows), own_rows)
        solved[0] = in_order(first[at, :], first_other[at, :], 1)
        solved[1] = in_order(second[at, :], second_other[at, :], 1)

    left, right = [], []
    for block in range(factor.shape[0]):
        at = pl.ds(block * depth, depth)
        for panel, (own, other) in enumerate(((first, first_other), (second, second_other))):
            left.append(factor[block, pl.ds(panel, rows, stride=2), :])
            right.append(jnp.concatenate([own[at, :], other[at, :]], axis=1))
    part = product(jnp.concatenate(left, axis=1), jnp.concatenate(right, axis=0))

    @pl.when(step == 0)
    def _():
        total[...] = part

    @pl.when(step > 0)
    def _():
        total[...] += part

    @pl.when(step == pl.num_programs(0) - 1)
    def _():
        half = out.shape[1] // 2
        out[...] = tail[...] - in_order(total[:, :half], total[:, half:], 1)


def params(mib):
    return pltpu.CompilerParams(vmem_limit_bytes=mib * 1024 * 1024)


def estimate(flops, size):
    return pl.CostEstimate(flops=flops, bytes_accessed=size, transcendentals=0)


def prepare(heads, cross):
    _, rows, columns = heads.shape
    chips = lax.axis_size("row") // CORES
    copies = jax.ShapeDtypeStruct((chips, CORES, rows, columns // CORES), jnp.float32)
    return pl.pallas_call(
        prepare_kernel,
        out_shape=(copies, copies, jax.ShapeDtypeStruct((chips,) + cross.shape, jnp.float32)),
        compiler_params=params(12),
        cost_estimate=estimate(0, 10 * (chips + 2) * rows * columns),
    )(heads, cross)


def on_chip(kernel, panel, own, other, operands, shapes, flops):
    _, rows, depth = own.shape
    inverse = pl.BlockSpec((1, rows, depth), lambda step: (panel, 0, 0))
    whole = lambda shape: pl.BlockSpec(shape, lambda step: (0,) * len(shape))
    size = 8 * rows * depth + 4 * sum(operand.size for operand in operands)
    return pl.pallas_call(
        kernel,
        grid=(1,),
        in_specs=[inverse, inverse] + [whole(operand.shape) for operand in operands],
        out_specs=[whole(shape) for shape in shapes],
        out_shape=[jax.ShapeDtypeStruct(shape, jnp.float32) for shape in shapes],
        compiler_params=params(20),
        cost_estimate=estimate(flops, size),
    )(own, other, *operands)


def tail_rows(tail, factor, halves):
    rows, columns = tail.shape
    blocks, double, width = factor.shape
    depth, half = halves[0].shape
    own_rows = depth // lax.axis_size("row")
    whole = lambda shape: pl.BlockSpec(shape, lambda step: (0,) * len(shape))
    shapes = [
        jax.ShapeDtypeStruct((rows, columns), jnp.float32),
        jax.ShapeDtypeStruct((2, own_rows, columns), jnp.float32),
    ]
    return pl.pallas_call(
        tail_kernel,
        grid=(TAIL_STEPS,),
        in_specs=[
            whole(tail.shape),
            pl.BlockSpec((blocks // TAIL_STEPS, double, width), lambda step: (step, 0, 0)),
        ]
        + [pl.BlockSpec((depth // TAIL_STEPS, half), lambda step: (step, 0)) for _ in halves],
        out_specs=[whole(shape.shape) for shape in shapes],
        out_shape=shapes,
        scratch_shapes=[pltpu.VMEM((rows, columns), jnp.float32)],
        compiler_params=params(55),
        cost_estimate=estimate(12 * rows * depth * columns, 4 * blocks * double * width),
    )(tail, factor, *halves)


def local(rhs_head, rhs_tail, diag_inv, factor_cross, factor_tail):
    rows, _, width = factor_tail.shape
    head_rows, depth = diag_inv.shape[1:]
    chips = lax.axis_size("row") // CORES
    chip_copies = (chips, CORES * head_rows, rhs_head.shape[2] // CORES)
    flops = 12 * head_rows * depth * chip_copies[2]

    factor = lax.all_gather(factor_tail.reshape(2 * rows, width), "col", axis=0)
    first_copies, second_copies, cross_copies = prepare(rhs_head, factor_cross)
    first_copies, cross_copies, inverse = lax.optimization_barrier((first_copies, cross_copies, diag_inv))
    cross = gather_chips(cross_copies).reshape(cross_copies.shape)
    first_head = gather_half(first_copies)
    inverse_other = swap(inverse)
    part = (head_rows, width)
    keep, send = on_chip(cross_kernel, 1, diag_inv, inverse_other, (cross,), (part, part), flops)
    product_rows = keep + swap(send)

    (first_copies,) = on_chip(solve_kernel, 0, diag_inv, inverse_other, (first_head,), (chip_copies,), flops)
    first_copies, second_copies, product_rows = lax.optimization_barrier(
        (first_copies, second_copies, product_rows)
    )
    first = gather_chips(first_copies)
    second_head = gather_half(second_copies)
    cross = lax.all_gather(product_rows, "col", axis=0)
    operands = (cross, swap(cross), second_head, first)
    (second_copies,) = on_chip(second_kernel, 1, diag_inv, inverse_other, operands, (chip_copies,), 2 * flops)
    second = gather_chips(second_copies)
    tail, solved = tail_rows(rhs_tail, factor, (first, swap(first), second, swap(second)))
    return solved, tail


def solution(mesh):
    return jax.shard_map(
        local,
        mesh=mesh,
        in_specs=(
            P(None, "row", "col"),
            P("row", "col"),
            P(None, "row", None),
            P("row", "col"),
            P("row", None, "col"),
        ),
        out_specs=(P(None, "row", "col"), P("row", "col")),
        check_vma=False,
    )
```

```python
import functools

import jax
import jax.numpy as jnp
from jax import lax
from jax.experimental import pallas as pl
from jax.experimental.pallas import tpu as pltpu
from jax.sharding import PartitionSpec as P

CORES = 2
TAIL_STEPS = 4


def swap(value):
    rows = lax.axis_size("row")
    return lax.ppermute(value, "row", [(i, i ^ 1) for i in range(rows)])


def gather_chips(copies):
    rows = lax.axis_size("row")
    groups = [list(range(core, rows, CORES)) for core in range(CORES)]
    blocks = lax.all_to_all(copies, "row", 0, 0, axis_index_groups=groups, tiled=True)
    return blocks.reshape(-1, blocks.shape[-1])


def gather_half(copies):
    chips, cores, rows, half = copies.shape
    return lax.all_to_all(copies.reshape(chips * cores, rows, half), "row", 0, 0, tiled=True).reshape(-1, half)


def pass_on(block, stride):
    rows, planes = lax.axis_size("row"), lax.axis_size("col")
    pairs = []
    for row in range(rows):
        turn = stride if row % CORES == 0 else -stride
        pairs += [(row * planes + z, row * planes + (z + turn) % planes) for z in range(planes)]
    return lax.ppermute(block, ("row", "col"), pairs)


def split(value):
    high = value.astype(jnp.bfloat16)
    low = (value - high.astype(jnp.float32)).astype(jnp.bfloat16)
    return high, low


def product(left, right):
    left_high, left_low = split(left)
    right_high, right_low = split(right)
    dot = functools.partial(jnp.dot, preferred_element_type=jnp.float32)
    return dot(left_high, right_high) + (dot(left_high, right_low) + dot(left_low, right_high))


def in_order(own, other, axis):
    first = lax.axis_index("row") % CORES == 0
    return jnp.concatenate([jnp.where(first, own, other), jnp.where(first, other, own)], axis=axis)


def spread(value, out):
    for chip in range(out.shape[0]):
        out[chip] = value


def prepare_kernel(heads, copies, keep, send):
    half = keep.shape[1]
    halves = [heads[0][:, core * half : (core + 1) * half] for core in range(CORES)]
    for chip in range(copies.shape[0]):
        for core in range(CORES):
            copies[chip, core] = halves[core]
    first = lax.axis_index("row") % CORES == 0
    left, right = heads[1][:, :half], heads[1][:, half:]
    keep[...] = jnp.where(first, left, right)
    send[...] = jnp.where(first, right, left)


def solve_kernel(own, other, operand, out):
    spread(product(in_order(own[0], other[0], 0), operand[...]), out)


def cross_kernel(head, head_other, operand, ring, out):
    planes, width = lax.axis_size("col"), ring.shape[2]
    here = lax.axis_index("col") + planes
    turn = 2 * (lax.axis_index("row") % CORES) - 1
    left, right = [], []
    for i in range(planes):
        plane = here + turn * i if i <= planes // 2 else here - turn * (i - planes // 2)
        left.append(ring[i])
        right.append(operand[pl.ds(pl.multiple_of(plane % planes * width, width), width), :])
    update = product(jnp.concatenate(left, axis=1), jnp.concatenate(right, axis=0))
    spread(in_order(head[...], head_other[...], 0) - update, out)


def tail_kernel(tail, factor, first, first_other, second, second_other, out, solved, total):
    step = pl.program_id(0)
    row = lax.axis_index("row")
    own_rows, depth, rows = solved.shape[1], factor.shape[2], out.shape[0]
    per_step = first.shape[0] // own_rows

    @pl.when(step == row // per_step)
    def _():
        at = pl.ds(pl.multiple_of((row % per_step) * own_rows, own_rows), own_rows)
        solved[0] = in_order(first[at, :], first_other[at, :], 1)
        solved[1] = in_order(second[at, :], second_other[at, :], 1)

    left, right = [], []
    for block in range(factor.shape[0]):
        at = pl.ds(block * depth, depth)
        for panel, (own, other) in enumerate(((first, first_other), (second, second_other))):
            left.append(factor[block, pl.ds(panel, rows, stride=2), :])
            right.append(jnp.concatenate([own[at, :], other[at, :]], axis=1))
    part = product(jnp.concatenate(left, axis=1), jnp.concatenate(right, axis=0))

    @pl.when(step == 0)
    def _():
        total[...] = part

    @pl.when(step > 0)
    def _():
        total[...] += part

    @pl.when(step == pl.num_programs(0) - 1)
    def _():
        half = out.shape[1] // 2
        out[...] = tail[...] - in_order(total[:, :half], total[:, half:], 1)


def params(mib):
    return pltpu.CompilerParams(vmem_limit_bytes=mib * 1024 * 1024)


def estimate(flops, size):
    return pl.CostEstimate(flops=flops, bytes_accessed=size, transcendentals=0)


def prepare(heads):
    _, rows, columns = heads.shape
    half = columns // CORES
    chips = lax.axis_size("row") // CORES
    part = jax.ShapeDtypeStruct((rows, half), jnp.float32)
    return pl.pallas_call(
        prepare_kernel,
        out_shape=(jax.ShapeDtypeStruct((chips, CORES, rows, half), jnp.float32), part, part),
        compiler_params=params(8),
        cost_estimate=estimate(0, 4 * (chips + 3) * rows * columns),
    )(heads)


def solve_chip(panel, own, other, operand):
    _, rows, depth = own.shape
    columns = operand.shape[1]
    chips = lax.axis_size("row") // CORES
    inverse = pl.BlockSpec((1, rows, depth), lambda step: (panel, 0, 0))
    shape = (chips, CORES * rows, columns)
    return pl.pallas_call(
        solve_kernel,
        grid=(1,),
        in_specs=[inverse, inverse, pl.BlockSpec(operand.shape, lambda step: (0, 0))],
        out_specs=pl.BlockSpec(shape, lambda step: (0, 0, 0)),
        out_shape=jax.ShapeDtypeStruct(shape, jnp.float32),
        compiler_params=params(16),
        cost_estimate=estimate(12 * rows * depth * columns, 4 * depth * (2 * rows + 2 * columns)),
    )(own, other, operand)


def cross_chip(head, head_other, operand, ring):
    rows = head.shape[0]
    depth, columns = operand.shape
    chips = lax.axis_size("row") // CORES
    return pl.pallas_call(
        cross_kernel,
        out_shape=jax.ShapeDtypeStruct((chips, CORES * rows, columns), jnp.float32),
        compiler_params=params(16),
        cost_estimate=estimate(12 * rows * depth * columns, 4 * depth * (2 * rows + 2 * columns)),
    )(head, head_other, operand, ring)


def tail_rows(tail, factor, halves):
    rows, columns = tail.shape
    blocks, double, width = factor.shape
    depth, half = halves[0].shape
    own_rows = depth // lax.axis_size("row")
    whole = lambda shape: pl.BlockSpec(shape, lambda step: (0,) * len(shape))
    shapes = [
        jax.ShapeDtypeStruct((rows, columns), jnp.float32),
        jax.ShapeDtypeStruct((2, own_rows, columns), jnp.float32),
    ]
    return pl.pallas_call(
        tail_kernel,
        grid=(TAIL_STEPS,),
        in_specs=[
            whole(tail.shape),
            pl.BlockSpec((blocks // TAIL_STEPS, double, width), lambda step: (step, 0, 0)),
        ]
        + [pl.BlockSpec((depth // TAIL_STEPS, half), lambda step: (step, 0)) for _ in halves],
        out_specs=[whole(shape.shape) for shape in shapes],
        out_shape=shapes,
        scratch_shapes=[pltpu.VMEM((rows, columns), jnp.float32)],
        compiler_params=params(55),
        cost_estimate=estimate(12 * rows * depth * columns, 4 * blocks * double * width),
    )(tail, factor, *halves)


def local(rhs_head, rhs_tail, diag_inv, factor_cross, factor_tail):
    rows, _, width = factor_tail.shape
    factor = lax.all_gather(factor_tail.reshape(2 * rows, width), "col", axis=0)
    copies, head, head_other = prepare(rhs_head)
    copies, diag_inv, factor_cross, head_other = lax.optimization_barrier(
        (copies, diag_inv, factor_cross, head_other)
    )
    first_head = gather_half(copies)
    inverse_other = swap(diag_inv)
    core = lax.axis_index("row") % CORES
    cross_other = swap(factor_cross)
    block = jnp.where(
        core == 0,
        jnp.concatenate([factor_cross, cross_other]),
        jnp.concatenate([cross_other, factor_cross]),
    )
    ring = [jnp.stack([pass_on(block, 1), pass_on(block, 2)])]
    first_head, ring[0] = lax.optimization_barrier((first_head, ring[0]))
    ring.append(pass_on(ring[-1], 2))
    first_copies = solve_chip(0, diag_inv, inverse_other, first_head)
    first_copies, head_other = lax.optimization_barrier((first_copies, head_other))
    first = gather_chips(first_copies)
    head_other = swap(head_other)
    while 2 * len(ring) < lax.axis_size("col") // 2:
        ring.append(pass_on(ring[-1], 2))
    near, far = jnp.concatenate(ring[:-1]), ring[-1]
    blocks = jnp.concatenate([block[None], near, far, swap(near), swap(far)])
    second_head = gather_chips(cross_chip(head, head_other, first, blocks))
    second = gather_chips(solve_chip(1, diag_inv, inverse_other, second_head))
    tail, solved = tail_rows(rhs_tail, factor, (first, swap(first), second, swap(second)))
    return solved, tail


def solution(mesh):
    return jax.shard_map(
        local,
        mesh=mesh,
        in_specs=(
            P(None, "row", "col"),
            P("row", "col"),
            P(None, "row", None),
            P("row", "col"),
            P("row", None, "col"),
        ),
        out_specs=(P(None, "row", "col"), P("row", "col")),
        check_vma=False,
    )
```

```python
import functools

import jax
import jax.numpy as jnp
from jax import lax
from jax.experimental import pallas as pl
from jax.experimental.pallas import tpu as pltpu
from jax.sharding import PartitionSpec as P

CORES = 2
TAIL_STEPS = 4


def swap(value):
    rows = lax.axis_size("row")
    return lax.ppermute(value, "row", [(i, i ^ 1) for i in range(rows)])


def gather_chips(copies):
    rows = lax.axis_size("row")
    groups = [list(range(core, rows, CORES)) for core in range(CORES)]
    blocks = lax.all_to_all(copies, "row", 0, 0, axis_index_groups=groups, tiled=True)
    return blocks.reshape(-1, blocks.shape[-1])


def gather_half(copies):
    chips, cores, rows, half = copies.shape
    return lax.all_to_all(copies.reshape(chips * cores, rows, half), "row", 0, 0, tiled=True).reshape(-1, half)


def split(value):
    high = value.astype(jnp.bfloat16)
    low = (value - high.astype(jnp.float32)).astype(jnp.bfloat16)
    return high, low


def product(left, right):
    left_high, left_low = split(left)
    right_high, right_low = split(right)
    dot = functools.partial(jnp.dot, preferred_element_type=jnp.float32)
    return dot(left_high, right_high) + (dot(left_high, right_low) + dot(left_low, right_high))


def in_order(own, other, axis):
    first = lax.axis_index("row") % CORES == 0
    return jnp.concatenate([jnp.where(first, own, other), jnp.where(first, other, own)], axis=axis)


def spread(value, out):
    for chip in range(out.shape[0]):
        out[chip] = value


def prepare_kernel(heads, copies, keep, send):
    half = keep.shape[1]
    halves = [heads[0][:, core * half : (core + 1) * half] for core in range(CORES)]
    for chip in range(copies.shape[0]):
        for core in range(CORES):
            copies[chip, core] = halves[core]
    first = lax.axis_index("row") % CORES == 0
    left, right = heads[1][:, :half], heads[1][:, half:]
    keep[...] = jnp.where(first, left, right)
    send[...] = jnp.where(first, right, left)


def fetch(sources, targets, sems):
    copies = [pltpu.make_async_copy(*pair, sems.at[i]) for i, pair in enumerate(zip(sources, targets))]
    for copy in copies:
        copy.start()

    def wait():
        for copy in copies:
            copy.wait()

    return wait


def product_of_parts(left, right_parts):
    high, low = split(left)
    right_high, right_low = right_parts
    dot = functools.partial(jnp.dot, preferred_element_type=jnp.float32)
    return dot(high, right_high) + (dot(high, right_low) + dot(low, right_high))


def solve_kernel(panel, inverse, inverse_other, operand, out, own, other, sems):
    wait = fetch((inverse.at[panel], inverse_other.at[panel]), (own, other), sems)
    right = split(operand[...])
    wait()
    spread(product_of_parts(in_order(own[...], other[...], 0), right), out)


def cross_kernel(cross, cross_other, head, head_other, operand, out, own, other, sems):
    wait = fetch((cross, cross_other), (own, other), sems)
    right = split(operand[...])
    wait()
    row_of = lambda blocks: jnp.concatenate([blocks[i] for i in range(blocks.shape[0])], axis=1)
    update = product_of_parts(in_order(row_of(own), row_of(other), 0), right)
    spread(in_order(head[...], head_other[...], 0) - update, out)


def own_rows_of(own, other, out, step):
    row, rows = lax.axis_index("row"), out.shape[0]
    per_step = own.shape[0] // rows

    @pl.when(step == row // per_step)
    def _():
        at = pl.ds(pl.multiple_of(row % per_step * rows, rows), rows)
        out[...] = in_order(own[at, :], other[at, :], 1)


def accumulate(tail, part, out, total, step):
    @pl.when(step == 0)
    def _():
        total[...] = part

    @pl.when(step > 0)
    def _():
        total[...] += part

    @pl.when(step == pl.num_programs(0) - 1)
    def _():
        half = out.shape[1] // 2
        out[...] = tail[...] - in_order(total[:, :half], total[:, half:], 1)


def first_tail_kernel(tail, factor, own, other, out, rows_out, high, low, total):
    step = pl.program_id(0)
    own_rows_of(own, other, rows_out, step)
    panel = lambda k: jnp.concatenate(
        [factor[i, pl.ds(k, out.shape[0], stride=2), :] for i in range(factor.shape[0])], axis=1
    )
    high[...], low[...] = split(panel(1))
    part = product(panel(0), jnp.concatenate([own[...], other[...]], axis=1))
    accumulate(tail, part, out, total, step)


def second_tail_kernel(tail, high, low, own, other, first_rows, out, solved, total):
    step = pl.program_id(0)
    own_rows_of(own, other, solved.at[1], step)

    @pl.when(step == 0)
    def _():
        solved[0] = first_rows[...]

    right_high, right_low = split(jnp.concatenate([own[...], other[...]], axis=1))
    dot = functools.partial(jnp.dot, preferred_element_type=jnp.float32)
    part = dot(high[...], right_high) + (dot(high[...], right_low) + dot(low[...], right_high))
    accumulate(tail, part, out, total, step)


def params(mib):
    return pltpu.CompilerParams(vmem_limit_bytes=mib * 1024 * 1024)


def estimate(flops, size):
    return pl.CostEstimate(flops=flops, bytes_accessed=size, transcendentals=0)


def prepare(heads):
    _, rows, columns = heads.shape
    half = columns // CORES
    chips = lax.axis_size("row") // CORES
    part = jax.ShapeDtypeStruct((rows, half), jnp.float32)
    return pl.pallas_call(
        prepare_kernel,
        out_shape=(jax.ShapeDtypeStruct((chips, CORES, rows, half), jnp.float32), part, part),
        compiler_params=params(8),
        cost_estimate=estimate(0, 4 * (chips + 3) * rows * columns),
    )(heads)


def on_chip(kernel, left, left_shape, others):
    depth, columns = others[-1].shape
    chips = lax.axis_size("row") // CORES
    rows = 2 * left_shape[-2]
    shape = (chips, rows, columns)
    return pl.pallas_call(
        kernel,
        in_specs=[pl.BlockSpec(memory_space=pl.ANY)] * 2 + [pl.BlockSpec(memory_space=pltpu.VMEM)] * len(others),
        out_shape=jax.ShapeDtypeStruct(shape, jnp.float32),
        scratch_shapes=[
            pltpu.VMEM(left_shape, jnp.float32),
            pltpu.VMEM(left_shape, jnp.float32),
            pltpu.SemaphoreType.DMA((2,)),
        ],
        compiler_params=params(20),
        cost_estimate=estimate(6 * rows * depth * columns, 4 * depth * (rows + 2 * columns)),
    )(*left, *others)


def solve_chip(panel, inverse, inverse_other, operand):
    kernel = functools.partial(solve_kernel, panel)
    return on_chip(kernel, (inverse, inverse_other), inverse.shape[1:], (operand,))


def cross_chip(cross, cross_other, head, head_other, operand):
    return on_chip(cross_kernel, (cross, cross_other), cross.shape, (head, head_other, operand))


def whole(shape):
    return pl.BlockSpec(shape, lambda step: (0,) * len(shape))


def first_tail(tail, factor, own, other):
    rows, columns = tail.shape
    blocks, double, width = factor.shape
    depth, half = own.shape
    own_rows = depth // lax.axis_size("row")
    part = pl.BlockSpec((depth // TAIL_STEPS, half), lambda step: (step, 0))
    parts = pl.BlockSpec((rows, depth // TAIL_STEPS), lambda step: (0, step))
    return pl.pallas_call(
        first_tail_kernel,
        grid=(TAIL_STEPS,),
        in_specs=[
            whole(tail.shape),
            pl.BlockSpec((blocks // TAIL_STEPS, double, width), lambda step: (step, 0, 0)),
            part,
            part,
        ],
        out_specs=[whole(tail.shape), whole((own_rows, columns)), parts, parts],
        out_shape=[
            jax.ShapeDtypeStruct(tail.shape, jnp.float32),
            jax.ShapeDtypeStruct((own_rows, columns), jnp.float32),
            jax.ShapeDtypeStruct((rows, depth), jnp.bfloat16),
            jax.ShapeDtypeStruct((rows, depth), jnp.bfloat16),
        ],
        scratch_shapes=[pltpu.VMEM((rows, columns), jnp.float32)],
        compiler_params=params(50),
        cost_estimate=estimate(6 * rows * depth * columns, 6 * blocks * double * width),
    )(tail, factor, own, other)


def second_tail(tail, high, low, own, other, first_rows):
    rows, columns = tail.shape
    depth, half = own.shape
    part = pl.BlockSpec((depth // TAIL_STEPS, half), lambda step: (step, 0))
    parts = pl.BlockSpec((rows, depth // TAIL_STEPS), lambda step: (0, step))
    shapes = (tail.shape, (2,) + first_rows.shape)
    return pl.pallas_call(
        second_tail_kernel,
        grid=(TAIL_STEPS,),
        in_specs=[whole(tail.shape), parts, parts, part, part, whole(first_rows.shape)],
        out_specs=[whole(shape) for shape in shapes],
        out_shape=[jax.ShapeDtypeStruct(shape, jnp.float32) for shape in shapes],
        scratch_shapes=[pltpu.VMEM((rows, columns), jnp.float32)],
        compiler_params=params(50),
        cost_estimate=estimate(6 * rows * depth * columns, 4 * rows * depth + 8 * depth * half),
    )(tail, high, low, own, other, first_rows)


def local(rhs_head, rhs_tail, diag_inv, factor_cross, factor_tail):
    rows, _, width = factor_tail.shape
    factor = lax.all_gather(factor_tail.reshape(2 * rows, width), "col", axis=0)
    copies, head, head_other = prepare(rhs_head)
    copies, diag_inv, factor_cross, head_other = lax.optimization_barrier(
        (copies, diag_inv, factor_cross, head_other)
    )
    first_head = gather_half(copies)
    inverse_other = swap(diag_inv)
    head_other = swap(head_other)
    cross = lax.all_gather(factor_cross, "col", axis=0)
    first_head, cross = lax.optimization_barrier((first_head, cross))
    cross_other = swap(cross)

    first = gather_chips(solve_chip(0, diag_inv, inverse_other, first_head))
    second_head = gather_chips(cross_chip(cross, cross_other, head, head_other, first))
    second_copies, first = lax.optimization_barrier((solve_chip(1, diag_inv, inverse_other, second_head), first))
    second = gather_chips(second_copies)
    first_other = swap(first)
    tail, first_rows, high, low = first_tail(rhs_tail, factor, first, first_other)
    second, tail, high, low = lax.optimization_barrier((second, tail, high, low))
    tail, solved = second_tail(tail, high, low, second, swap(second), first_rows)
    return solved, tail


def solution(mesh):
    return jax.shard_map(
        local,
        mesh=mesh,
        in_specs=(
            P(None, "row", "col"),
            P("row", "col"),
            P(None, "row", None),
            P("row", "col"),
            P("row", None, "col"),
        ),
        out_specs=(P(None, "row", "col"), P("row", "col")),
        check_vma=False,
    )
```

```python
import functools

import jax
import jax.numpy as jnp
from jax import lax
from jax.experimental import pallas as pl
from jax.experimental.pallas import tpu as pltpu
from jax.sharding import PartitionSpec as P

CORES = 2
TAIL_STEPS = 4


def swap(value):
    rows = lax.axis_size("row")
    return lax.ppermute(value, "row", [(i, i ^ 1) for i in range(rows)])


def gather_cores(value):
    rows = lax.axis_size("row")
    pairs = [list(range(i, i + CORES)) for i in range(0, rows, CORES)]
    return lax.all_gather(value, "row", axis=0, axis_index_groups=pairs)


def gather_chips(copies):
    rows = lax.axis_size("row")
    groups = [list(range(core, rows, CORES)) for core in range(CORES)]
    blocks = lax.all_to_all(copies, "row", 0, 0, axis_index_groups=groups, tiled=True)
    return blocks.reshape(-1, blocks.shape[-1])


def gather_half(copies):
    chips, cores, rows, half = copies.shape
    return lax.all_to_all(copies.reshape(chips * cores, rows, half), "row", 0, 0, tiled=True).reshape(-1, half)


def split(value):
    high = value.astype(jnp.bfloat16)
    low = (value - high.astype(jnp.float32)).astype(jnp.bfloat16)
    return high, low


def product(left, right):
    left_high, left_low = split(left)
    right_high, right_low = split(right)
    dot = functools.partial(jnp.dot, preferred_element_type=jnp.float32)
    return dot(left_high, right_high) + (dot(left_high, right_low) + dot(left_low, right_high))


def in_order(own, other, axis):
    first = lax.axis_index("row") % CORES == 0
    return jnp.concatenate([jnp.where(first, own, other), jnp.where(first, other, own)], axis=axis)


def spread(value, out):
    for chip in range(out.shape[0]):
        out[chip] = value


def prepare_kernel(heads, copies, keep, send):
    half = keep.shape[1]
    halves = [heads[0][:, core * half : (core + 1) * half] for core in range(CORES)]
    for chip in range(copies.shape[0]):
        for core in range(CORES):
            copies[chip, core] = halves[core]
    first = lax.axis_index("row") % CORES == 0
    left, right = heads[1][:, :half], heads[1][:, half:]
    keep[...] = jnp.where(first, left, right)
    send[...] = jnp.where(first, right, left)


def fetch(sources, targets, sems):
    copies = [pltpu.make_async_copy(*pair, sems.at[i]) for i, pair in enumerate(zip(sources, targets))]
    for copy in copies:
        copy.start()

    def wait():
        for copy in copies:
            copy.wait()

    return wait


def product_of_parts(left, right_parts):
    high, low = split(left)
    right_high, right_low = right_parts
    dot = functools.partial(jnp.dot, preferred_element_type=jnp.float32)
    return dot(high, right_high) + (dot(high, right_low) + dot(low, right_high))


def solve_kernel(panel, inverse, operand, out, left, sems):
    rows = inverse.shape[2]
    targets = [left.at[pl.ds(core * rows, rows), :] for core in range(CORES)]
    wait = fetch([inverse.at[core, panel] for core in range(CORES)], targets, sems)
    right = split(operand[...])
    wait()
    spread(product_of_parts(left[...], right), out)


def cross_kernel(cross, cross_other, head, head_other, operand, out, own, other, sems):
    wait = fetch((cross, cross_other), (own, other), sems)
    right = split(operand[...])
    wait()
    row_of = lambda blocks: jnp.concatenate([blocks[i] for i in range(blocks.shape[0])], axis=1)
    update = product_of_parts(in_order(row_of(own), row_of(other), 0), right)
    spread(in_order(head[...], head_other[...], 0) - update, out)


def tail_kernel(tail, factor, first, first_other, second, second_other, out, solved, total):
    step = pl.program_id(0)
    row = lax.axis_index("row")
    own_rows, depth, rows = solved.shape[1], factor.shape[2], out.shape[0]
    per_step = first.shape[0] // own_rows

    @pl.when(step == row // per_step)
    def _():
        at = pl.ds(pl.multiple_of((row % per_step) * own_rows, own_rows), own_rows)
        solved[0] = in_order(first[at, :], first_other[at, :], 1)
        solved[1] = in_order(second[at, :], second_other[at, :], 1)

    left, right = [], []
    for block in range(factor.shape[0]):
        at = pl.ds(block * depth, depth)
        for panel, (own, other) in enumerate(((first, first_other), (second, second_other))):
            left.append(factor[block, pl.ds(panel, rows, stride=2), :])
            right.append(jnp.concatenate([own[at, :], other[at, :]], axis=1))
    part = product(jnp.concatenate(left, axis=1), jnp.concatenate(right, axis=0))

    @pl.when(step == 0)
    def _():
        total[...] = part

    @pl.when(step > 0)
    def _():
        total[...] += part

    @pl.when(step == pl.num_programs(0) - 1)
    def _():
        half = out.shape[1] // 2
        out[...] = tail[...] - in_order(total[:, :half], total[:, half:], 1)


def params(mib):
    return pltpu.CompilerParams(vmem_limit_bytes=mib * 1024 * 1024)


def estimate(flops, size):
    return pl.CostEstimate(flops=flops, bytes_accessed=size, transcendentals=0)


def prepare(heads):
    _, rows, columns = heads.shape
    half = columns // CORES
    chips = lax.axis_size("row") // CORES
    part = jax.ShapeDtypeStruct((rows, half), jnp.float32)
    return pl.pallas_call(
        prepare_kernel,
        out_shape=(jax.ShapeDtypeStruct((chips, CORES, rows, half), jnp.float32), part, part),
        compiler_params=params(8),
        cost_estimate=estimate(0, 4 * (chips + 3) * rows * columns),
    )(heads)


def on_chip(kernel, lefts, scratch, others):
    depth, columns = others[-1].shape
    chips = lax.axis_size("row") // CORES
    shape = (chips, depth // chips, columns)
    return pl.pallas_call(
        kernel,
        in_specs=[pl.BlockSpec(memory_space=pl.ANY)] * len(lefts)
        + [pl.BlockSpec(memory_space=pltpu.VMEM)] * len(others),
        out_shape=jax.ShapeDtypeStruct(shape, jnp.float32),
        scratch_shapes=[pltpu.VMEM(of, jnp.float32) for of in scratch] + [pltpu.SemaphoreType.DMA((2,))],
        compiler_params=params(20),
        cost_estimate=estimate(6 * shape[1] * depth * columns, 4 * depth * (shape[1] + 2 * columns)),
    )(*lefts, *others)


def solve_chip(panel, inverse, operand):
    _, _, rows, depth = inverse.shape
    kernel = functools.partial(solve_kernel, panel)
    return on_chip(kernel, (inverse,), ((CORES * rows, depth),), (operand,))


def cross_chip(cross, cross_other, head, head_other, operand):
    return on_chip(cross_kernel, (cross, cross_other), (cross.shape,) * 2, (head, head_other, operand))


def tail_rows(tail, factor, halves):
    rows, columns = tail.shape
    blocks, double, width = factor.shape
    depth, half = halves[0].shape
    own_rows = depth // lax.axis_size("row")
    whole = lambda shape: pl.BlockSpec(shape, lambda step: (0,) * len(shape))
    shapes = [
        jax.ShapeDtypeStruct((rows, columns), jnp.float32),
        jax.ShapeDtypeStruct((2, own_rows, columns), jnp.float32),
    ]
    return pl.pallas_call(
        tail_kernel,
        grid=(TAIL_STEPS,),
        in_specs=[
            whole(tail.shape),
            pl.BlockSpec((blocks // TAIL_STEPS, double, width), lambda step: (step, 0, 0)),
        ]
        + [pl.BlockSpec((depth // TAIL_STEPS, half), lambda step: (step, 0)) for _ in halves],
        out_specs=[whole(shape.shape) for shape in shapes],
        out_shape=shapes,
        scratch_shapes=[pltpu.VMEM((rows, columns), jnp.float32)],
        compiler_params=params(55),
        cost_estimate=estimate(12 * rows * depth * columns, 4 * blocks * double * width),
    )(tail, factor, *halves)


def local(rhs_head, rhs_tail, diag_inv, factor_cross, factor_tail):
    rows, _, width = factor_tail.shape
    inverse = gather_cores(diag_inv)
    copies, head, head_other = prepare(rhs_head)
    copies, factor_cross, head_other, factor_tail = lax.optimization_barrier(
        (copies, factor_cross, head_other, factor_tail)
    )
    factor = lax.all_gather(factor_tail.reshape(2 * rows, width), "col", axis=0)
    first_head = gather_half(copies)
    head_other = swap(head_other)
    cross = lax.all_gather(factor_cross, "col", axis=0)
    first_head, cross = lax.optimization_barrier((first_head, cross))
    cross_other = swap(cross)

    first = gather_chips(solve_chip(0, inverse, first_head))
    second_head = gather_chips(cross_chip(cross, cross_other, head, head_other, first))
    second = gather_chips(solve_chip(1, inverse, second_head))
    tail, solved = tail_rows(rhs_tail, factor, (first, swap(first), second, swap(second)))
    return solved, tail


def solution(mesh):
    return jax.shard_map(
        local,
        mesh=mesh,
        in_specs=(
            P(None, "row", "col"),
            P("row", "col"),
            P(None, "row", None),
            P("row", "col"),
            P("row", None, "col"),
        ),
        out_specs=(P(None, "row", "col"), P("row", "col")),
        check_vma=False,
    )
```

```python
import functools

import jax
import jax.numpy as jnp
from jax import lax
from jax.experimental import pallas as pl
from jax.experimental.pallas import tpu as pltpu
from jax.sharding import PartitionSpec as P

CORES = 2
TAIL_STEPS = 4


def swap(value):
    rows = lax.axis_size("row")
    return lax.ppermute(value, "row", [(i, i ^ 1) for i in range(rows)])


def gather_cores(value):
    rows = lax.axis_size("row")
    pairs = [list(range(i, i + CORES)) for i in range(0, rows, CORES)]
    return lax.all_gather(value, "row", axis=0, axis_index_groups=pairs)


def gather_chips(copies):
    rows = lax.axis_size("row")
    groups = [list(range(core, rows, CORES)) for core in range(CORES)]
    blocks = lax.all_to_all(copies, "row", 0, 0, axis_index_groups=groups, tiled=True)
    return blocks.reshape(-1, blocks.shape[-1])


def gather_half(copies):
    chips, cores, rows, half = copies.shape
    return lax.all_to_all(copies.reshape(chips * cores, rows, half), "row", 0, 0, tiled=True).reshape(-1, half)


def split(value):
    high = value.astype(jnp.bfloat16)
    low = (value - high.astype(jnp.float32)).astype(jnp.bfloat16)
    return high, low


def product(left, right):
    left_high, left_low = split(left)
    right_high, right_low = split(right)
    dot = functools.partial(jnp.dot, preferred_element_type=jnp.float32)
    return dot(left_high, right_high) + (dot(left_high, right_low) + dot(left_low, right_high))


def in_order(own, other, axis):
    first = lax.axis_index("row") % CORES == 0
    return jnp.concatenate([jnp.where(first, own, other), jnp.where(first, other, own)], axis=axis)


def spread(value, out):
    for chip in range(out.shape[0]):
        out[chip] = value


def prepare_kernel(heads, copies, keep, send):
    half = keep.shape[1]
    halves = [heads[0][:, core * half : (core + 1) * half] for core in range(CORES)]
    for chip in range(copies.shape[0]):
        for core in range(CORES):
            copies[chip, core] = halves[core]
    first = lax.axis_index("row") % CORES == 0
    left, right = heads[1][:, :half], heads[1][:, half:]
    keep[...] = jnp.where(first, left, right)
    send[...] = jnp.where(first, right, left)


def fetch(sources, targets, sems):
    copies = [pltpu.make_async_copy(*pair, sems.at[i]) for i, pair in enumerate(zip(sources, targets))]
    for copy in copies:
        copy.start()

    def wait():
        for copy in copies:
            copy.wait()

    return wait


def product_of_parts(left, right_parts):
    high, low = split(left)
    right_high, right_low = right_parts
    dot = functools.partial(jnp.dot, preferred_element_type=jnp.float32)
    return dot(high, right_high) + (dot(high, right_low) + dot(low, right_high))


def first_kernel(inverse, operand, out, own, other, sems):
    wait = fetch([inverse.at[core] for core in range(CORES)], (own, other), sems)
    right = split(operand[...])
    wait()
    spread(product_of_parts(jnp.concatenate([own[...], other[...]], axis=0), right), out)


def second_kernel(inverse, inverse_other, operand, out, own, other, sems):
    wait = fetch((inverse.at[1], inverse_other), (own, other), sems)
    right = split(operand[...])
    wait()
    spread(product_of_parts(in_order(own[...], other[...], 0), right), out)


def cross_kernel(cross, cross_other, head, head_other, operand, out, own, other, sems):
    wait = fetch((cross, cross_other), (own, other), sems)
    right = split(operand[...])
    wait()
    row_of = lambda blocks: jnp.concatenate([blocks[i] for i in range(blocks.shape[0])], axis=1)
    update = product_of_parts(in_order(row_of(own), row_of(other), 0), right)
    spread(in_order(head[...], head_other[...], 0) - update, out)


def tail_kernel(tail, factor, first, first_other, second, second_other, out, solved, total):
    step = pl.program_id(0)
    row = lax.axis_index("row")
    own_rows, depth, rows = solved.shape[1], factor.shape[2], out.shape[0]
    per_step = first.shape[0] // own_rows

    @pl.when(step == row // per_step)
    def _():
        at = pl.ds(pl.multiple_of((row % per_step) * own_rows, own_rows), own_rows)
        solved[0] = in_order(first[at, :], first_other[at, :], 1)
        solved[1] = in_order(second[at, :], second_other[at, :], 1)

    left, right = [], []
    for block in range(factor.shape[0]):
        at = pl.ds(block * depth, depth)
        for panel, (own, other) in enumerate(((first, first_other), (second, second_other))):
            left.append(factor[block, pl.ds(panel, rows, stride=2), :])
            right.append(jnp.concatenate([own[at, :], other[at, :]], axis=1))
    part = product(jnp.concatenate(left, axis=1), jnp.concatenate(right, axis=0))

    @pl.when(step == 0)
    def _():
        total[...] = part

    @pl.when(step > 0)
    def _():
        total[...] += part

    @pl.when(step == pl.num_programs(0) - 1)
    def _():
        half = out.shape[1] // 2
        out[...] = tail[...] - in_order(total[:, :half], total[:, half:], 1)


def params(mib):
    return pltpu.CompilerParams(vmem_limit_bytes=mib * 1024 * 1024)


def estimate(flops, size):
    return pl.CostEstimate(flops=flops, bytes_accessed=size, transcendentals=0)


def prepare(heads):
    _, rows, columns = heads.shape
    half = columns // CORES
    chips = lax.axis_size("row") // CORES
    part = jax.ShapeDtypeStruct((rows, half), jnp.float32)
    return pl.pallas_call(
        prepare_kernel,
        out_shape=(jax.ShapeDtypeStruct((chips, CORES, rows, half), jnp.float32), part, part),
        compiler_params=params(8),
        cost_estimate=estimate(0, 4 * (chips + 3) * rows * columns),
    )(heads)


def on_chip(kernel, lefts, scratch, others):
    depth, columns = others[-1].shape
    chips = lax.axis_size("row") // CORES
    shape = (chips, depth // chips, columns)
    return pl.pallas_call(
        kernel,
        in_specs=[pl.BlockSpec(memory_space=pl.ANY)] * len(lefts)
        + [pl.BlockSpec(memory_space=pltpu.VMEM)] * len(others),
        out_shape=jax.ShapeDtypeStruct(shape, jnp.float32),
        scratch_shapes=[pltpu.VMEM(of, jnp.float32) for of in scratch] + [pltpu.SemaphoreType.DMA((2,))],
        compiler_params=params(20),
        cost_estimate=estimate(6 * shape[1] * depth * columns, 4 * depth * (shape[1] + 2 * columns)),
    )(*lefts, *others)


def cross_chip(cross, cross_other, head, head_other, operand):
    return on_chip(cross_kernel, (cross, cross_other), (cross.shape,) * 2, (head, head_other, operand))


def tail_rows(tail, factor, halves):
    rows, columns = tail.shape
    blocks, double, width = factor.shape
    depth, half = halves[0].shape
    own_rows = depth // lax.axis_size("row")
    whole = lambda shape: pl.BlockSpec(shape, lambda step: (0,) * len(shape))
    shapes = [
        jax.ShapeDtypeStruct((rows, columns), jnp.float32),
        jax.ShapeDtypeStruct((2, own_rows, columns), jnp.float32),
    ]
    return pl.pallas_call(
        tail_kernel,
        grid=(TAIL_STEPS,),
        in_specs=[
            whole(tail.shape),
            pl.BlockSpec((blocks // TAIL_STEPS, double, width), lambda step: (step, 0, 0)),
        ]
        + [pl.BlockSpec((depth // TAIL_STEPS, half), lambda step: (step, 0)) for _ in halves],
        out_specs=[whole(shape.shape) for shape in shapes],
        out_shape=shapes,
        scratch_shapes=[pltpu.VMEM((rows, columns), jnp.float32)],
        compiler_params=params(55),
        cost_estimate=estimate(12 * rows * depth * columns, 4 * blocks * double * width),
    )(tail, factor, *halves)


def local(rhs_head, rhs_tail, diag_inv, factor_cross, factor_tail):
    rows, _, width = factor_tail.shape
    inverse = gather_cores(diag_inv[0])
    copies, head, head_other = prepare(rhs_head)
    copies, factor_cross, head_other, factor_tail = lax.optimization_barrier(
        (copies, factor_cross, head_other, factor_tail)
    )
    factor = lax.all_gather(factor_tail.reshape(2 * rows, width), "col", axis=0)
    first_head = gather_half(copies)
    head_other = swap(head_other)
    cross = lax.all_gather(factor_cross, "col", axis=0)
    first_head, cross = lax.optimization_barrier((first_head, cross))
    cross_other = swap(cross)

    both = (diag_inv.shape[1:],) * 2
    first_copies = on_chip(first_kernel, (inverse,), both, (first_head,))
    first_copies, second_inverse = lax.optimization_barrier((first_copies, diag_inv[1]))
    first = gather_chips(first_copies)
    inverse_other = swap(second_inverse)
    second_head = gather_chips(cross_chip(cross, cross_other, head, head_other, first))
    second = gather_chips(on_chip(second_kernel, (diag_inv, inverse_other), both, (second_head,)))
    tail, solved = tail_rows(rhs_tail, factor, (first, swap(first), second, swap(second)))
    return solved, tail


def solution(mesh):
    return jax.shard_map(
        local,
        mesh=mesh,
        in_specs=(
            P(None, "row", "col"),
            P("row", "col"),
            P(None, "row", None),
            P("row", "col"),
            P("row", None, "col"),
        ),
        out_specs=(P(None, "row", "col"), P("row", "col")),
        check_vma=False,
    )
```

```python
import functools

import jax
import jax.numpy as jnp
from jax import lax
from jax.experimental import pallas as pl
from jax.experimental.pallas import tpu as pltpu
from jax.sharding import PartitionSpec as P

CORES = 2
TAIL_STEPS = 4


def swap(value):
    rows = lax.axis_size("row")
    return lax.ppermute(value, "row", [(i, i ^ 1) for i in range(rows)])


def gather_chips(copies):
    rows = lax.axis_size("row")
    groups = [list(range(core, rows, CORES)) for core in range(CORES)]
    blocks = lax.all_to_all(copies, "row", 0, 0, axis_index_groups=groups, tiled=True)
    return blocks.reshape(-1, blocks.shape[-1])


def gather_half(copies):
    chips, cores, rows, half = copies.shape
    return lax.all_to_all(copies.reshape(chips * cores, rows, half), "row", 0, 0, tiled=True).reshape(-1, half)


def split(value):
    high = value.astype(jnp.bfloat16)
    low = (value - high.astype(jnp.float32)).astype(jnp.bfloat16)
    return high, low


def product(left, right):
    left_high, left_low = split(left)
    right_high, right_low = split(right)
    dot = functools.partial(jnp.dot, preferred_element_type=jnp.float32)
    return dot(left_high, right_high) + (dot(left_high, right_low) + dot(left_low, right_high))


def in_order(own, other, axis):
    first = lax.axis_index("row") % CORES == 0
    return jnp.concatenate([jnp.where(first, own, other), jnp.where(first, other, own)], axis=axis)


def spread(value, out):
    for chip in range(out.shape[0]):
        out[chip] = value


def prepare_kernel(heads, copies, keep, send):
    half = keep.shape[1]
    halves = [heads[0][:, core * half : (core + 1) * half] for core in range(CORES)]
    for chip in range(copies.shape[0]):
        for core in range(CORES):
            copies[chip, core] = halves[core]
    first = lax.axis_index("row") % CORES == 0
    left, right = heads[1][:, :half], heads[1][:, half:]
    keep[...] = jnp.where(first, left, right)
    send[...] = jnp.where(first, right, left)


def fetch(sources, targets, sems):
    copies = [pltpu.make_async_copy(*pair, sems.at[i]) for i, pair in enumerate(zip(sources, targets))]
    for copy in copies:
        copy.start()

    def wait():
        for copy in copies:
            copy.wait()

    return wait


def product_of_parts(left, right_parts):
    high, low = split(left)
    right_high, right_low = right_parts
    dot = functools.partial(jnp.dot, preferred_element_type=jnp.float32)
    return dot(high, right_high) + (dot(high, right_low) + dot(low, right_high))


def solve_kernel(panel, inverse, inverse_other, operand, out, own, other, sems):
    wait = fetch((inverse.at[panel], inverse_other.at[panel]), (own, other), sems)
    right = split(operand[...])
    wait()
    spread(product_of_parts(in_order(own[...], other[...], 0), right), out)


def cross_kernel(cross, cross_other, head, head_other, operand, out, own, other, sems):
    wait = fetch((cross, cross_other), (own, other), sems)
    right = split(operand[...])
    wait()
    row_of = lambda blocks: jnp.concatenate([blocks[i] for i in range(blocks.shape[0])], axis=1)
    update = product_of_parts(in_order(row_of(own), row_of(other), 0), right)
    spread(in_order(head[...], head_other[...], 0) - update, out)


def tail_kernel(tail, factor, first, first_other, second, second_other, out, solved, total):
    step = pl.program_id(0)
    row = lax.axis_index("row")
    own_rows, depth, rows = solved.shape[1], factor.shape[2], out.shape[0]
    per_step = first.shape[0] // own_rows

    @pl.when(step == row // per_step)
    def _():
        at = pl.ds(pl.multiple_of((row % per_step) * own_rows, own_rows), own_rows)
        solved[0] = in_order(first[at, :], first_other[at, :], 1)
        solved[1] = in_order(second[at, :], second_other[at, :], 1)

    left, right = [], []
    for block in range(factor.shape[0]):
        at = pl.ds(block * depth, depth)
        for panel, (own, other) in enumerate(((first, first_other), (second, second_other))):
            left.append(factor[block, pl.ds(panel, rows, stride=2), :])
            right.append(jnp.concatenate([own[at, :], other[at, :]], axis=1))
    part = product(jnp.concatenate(left, axis=1), jnp.concatenate(right, axis=0))

    @pl.when(step == 0)
    def _():
        total[...] = part

    @pl.when(step > 0)
    def _():
        total[...] += part

    @pl.when(step == pl.num_programs(0) - 1)
    def _():
        half = out.shape[1] // 2
        out[...] = tail[...] - in_order(total[:, :half], total[:, half:], 1)


def params(mib):
    return pltpu.CompilerParams(vmem_limit_bytes=mib * 1024 * 1024)


def estimate(flops, size):
    return pl.CostEstimate(flops=flops, bytes_accessed=size, transcendentals=0)


def prepare(heads):
    _, rows, columns = heads.shape
    half = columns // CORES
    chips = lax.axis_size("row") // CORES
    part = jax.ShapeDtypeStruct((rows, half), jnp.float32)
    return pl.pallas_call(
        prepare_kernel,
        out_shape=(jax.ShapeDtypeStruct((chips, CORES, rows, half), jnp.float32), part, part),
        compiler_params=params(8),
        cost_estimate=estimate(0, 4 * (chips + 3) * rows * columns),
    )(heads)


def on_chip(kernel, left, left_shape, others):
    depth, columns = others[-1].shape
    chips = lax.axis_size("row") // CORES
    rows = 2 * left_shape[-2]
    shape = (chips, rows, columns)
    return pl.pallas_call(
        kernel,
        in_specs=[pl.BlockSpec(memory_space=pl.ANY)] * 2 + [pl.BlockSpec(memory_space=pltpu.VMEM)] * len(others),
        out_shape=jax.ShapeDtypeStruct(shape, jnp.float32),
        scratch_shapes=[
            pltpu.VMEM(left_shape, jnp.float32),
            pltpu.VMEM(left_shape, jnp.float32),
            pltpu.SemaphoreType.DMA((2,)),
        ],
        compiler_params=params(20),
        cost_estimate=estimate(6 * rows * depth * columns, 4 * depth * (rows + 2 * columns)),
    )(*left, *others)


def solve_chip(panel, inverse, inverse_other, operand):
    kernel = functools.partial(solve_kernel, panel)
    return on_chip(kernel, (inverse, inverse_other), inverse.shape[1:], (operand,))


def cross_chip(cross, cross_other, head, head_other, operand):
    return on_chip(cross_kernel, (cross, cross_other), cross.shape, (head, head_other, operand))


def tail_rows(tail, factor, halves):
    rows, columns = tail.shape
    blocks, double, width = factor.shape
    depth, half = halves[0].shape
    own_rows = depth // lax.axis_size("row")
    whole = lambda shape: pl.BlockSpec(shape, lambda step: (0,) * len(shape))
    shapes = [
        jax.ShapeDtypeStruct((rows, columns), jnp.float32),
        jax.ShapeDtypeStruct((2, own_rows, columns), jnp.float32),
    ]
    return pl.pallas_call(
        tail_kernel,
        grid=(TAIL_STEPS,),
        in_specs=[
            whole(tail.shape),
            pl.BlockSpec((blocks // TAIL_STEPS, double, width), lambda step: (step, 0, 0)),
        ]
        + [pl.BlockSpec((depth // TAIL_STEPS, half), lambda step: (step, 0)) for _ in halves],
        out_specs=[whole(shape.shape) for shape in shapes],
        out_shape=shapes,
        scratch_shapes=[pltpu.VMEM((rows, columns), jnp.float32)],
        compiler_params=params(55),
        cost_estimate=estimate(12 * rows * depth * columns, 4 * blocks * double * width),
    )(tail, factor, *halves)


def local(rhs_head, rhs_tail, diag_inv, factor_cross, factor_tail):
    rows, _, width = factor_tail.shape
    copies, head, head_other = prepare(rhs_head)
    copies, diag_inv, factor_cross, head_other, factor_tail = lax.optimization_barrier(
        (copies, diag_inv, factor_cross, head_other, factor_tail)
    )
    factor = lax.all_gather(factor_tail.reshape(2 * rows, width), "col", axis=0)
    first_head = gather_half(copies)
    inverse_other = swap(diag_inv)
    head_other = swap(head_other)
    cross = lax.all_gather(factor_cross, "col", axis=0)
    first_head, cross = lax.optimization_barrier((first_head, cross))
    cross_other = swap(cross)

    first = gather_chips(solve_chip(0, diag_inv, inverse_other, first_head))
    second_head = gather_chips(cross_chip(cross, cross_other, head, head_other, first))
    second = gather_chips(solve_chip(1, diag_inv, inverse_other, second_head))
    tail, solved = tail_rows(rhs_tail, factor, (first, swap(first), second, swap(second)))
    return solved, tail


def solution(mesh):
    return jax.shard_map(
        local,
        mesh=mesh,
        in_specs=(
            P(None, "row", "col"),
            P("row", "col"),
            P(None, "row", None),
            P("row", "col"),
            P("row", None, "col"),
        ),
        out_specs=(P(None, "row", "col"), P("row", "col")),
        check_vma=False,
    )
```
